32 devices in a mesh: tm: 4 (over y, x), height: 2 (over core), head: 4 (over z).
Axes of the slice: x: 2, y: 2, z: 4, core: 2. Of those that a mesh axis runs over, the one named last changes fastest.
Arguments:
- queries: bfloat16 [4, 2, 128, 3072], P('tm', 'height', None, 'head'), may hold values from -8 to 8
- keys: bfloat16 [4, 2, 128, 3072], P('tm', 'height', None, 'head'), may hold values from -8 to 8
- values: bfloat16 [4, 2, 128, 3072], P('tm', 'height', None, 'head'), may hold values from -6 to 6
- grad_out: bfloat16 [4, 2, 128, 3072], P('tm', 'height', None, 'head'), may hold values from -6 to 6
- caption_keys: bfloat16 [256, 3072], P(None, 'head'), may hold values from -6 to 6
- caption_values: bfloat16 [256, 3072], P(None, 'head'), may hold values from -6 to 6
- caption_mask: int32 [256], replicated, may hold values 0 or 1
- kept: int32 [4, 2, 4], P('tm', 'height'), may hold values 0 or 1
Outputs:
- attended: bfloat16 [4, 2, 128, 3072], P('tm', 'height', None, 'head')
- query_grad: bfloat16 [4, 2, 128, 3072], P('tm', 'height', None, 'head')
- key_grad: bfloat16 [4, 2, 128, 3072], P('tm', 'height', None, 'head')
- value_grad: bfloat16 [4, 2, 128, 3072], P('tm', 'height', None, 'head')
- caption_key_grad: bfloat16 [256, 3072], P(None, 'head')
- caption_value_grad: bfloat16 [256, 3072], P(None, 'head')
The draws below stay inside these ranges and needn't reach their ends.
All inputs are finite; a program needn't handle non-finite values. No bound on the sum of `kept` on one device may be relied on, other than what follows from the above.
Results may differ from the reference program's by a relative error of at most 0.029.
Values may be sent and summed in bfloat16 or wider, within the bound.
A program may use at most 64 MiB of HBM per device.

```python
import math
import jax
import jax.numpy as jnp
from jax import lax

D = 3072
HEADS = 24
HD = 128
TILE = 128
CAP = 256
NT = 4
NH = 2


def base_draw(key):
    return jnp.clip(jax.random.normal(key, (NT, NH, TILE, D), jnp.float32), -6.0, 6.0)


def draw_queries(key, part):
    result = base_draw(jax.random.fold_in(key, 21))
    return result.astype(jnp.bfloat16)


def draw_keys(key, part):
    result = base_draw(jax.random.fold_in(key, 22))
    return result.astype(jnp.bfloat16)


def with_ends(drawn, stream_key, least, top_value):
    place = [jax.random.randint(jax.random.fold_in(stream_key, axis), (), 0, length) for axis, length in enumerate(drawn.shape)]
    widest = drawn.shape.index(max(drawn.shape))
    next_to = place[:widest] + [(place[widest] + 1) % drawn.shape[widest]] + place[widest + 1:]
    return drawn.at[tuple(place)].set(least).at[tuple(next_to)].set(top_value)


def steps_of(stream_key, shape, pieces, least, high):
    factor_of, own = 1.0, jax.random.fold_in(stream_key, 6)
    for axis_at, shards_of in pieces:
        draws = jnp.exp(jax.random.uniform(jax.random.fold_in(own, axis_at), (shards_of,), jnp.float32, least / len(pieces), high / len(pieces)))
        factor_of = factor_of * jnp.repeat(draws, shape[axis_at] // shards_of).reshape([-1 if axis == axis_at else 1 for axis in range(len(shape))])
    return factor_of


def bell_draw(key, extent, spread, limit, shards=(), kind=jnp.bfloat16):
    gain = steps_of(key, extent, shards, -0.22, 0.18) if shards else 1.0
    values = jax.random.normal(key, extent, jnp.float32) * spread * gain
    return jnp.minimum(jnp.maximum(values, -limit), limit).astype(kind)


def setup_inputs(seed: int = 0) -> dict:
    seeds = jax.random.split(jax.random.key(seed), 9)
    queries = draw_queries(jax.random.fold_in(seeds[8], 71), 0)
    keys = draw_keys(jax.random.fold_in(seeds[8], 71), 0)
    values = bell_draw(seeds[2], (NT, NH, TILE, D), 1.0, 6.0, ((0, 4), (1, 2), (3, 4)))
    grad_out = bell_draw(seeds[3], (NT, NH, TILE, D), 1.0, 6.0, ((0, 4), (1, 2), (3, 4)))
    caption_keys = bell_draw(seeds[4], (CAP, D), 1.0, 6.0, ((1, 4),))
    caption_values = bell_draw(seeds[5], (CAP, D), 1.0, 6.0, ((1, 4),))
    caption_mask = with_ends((jax.random.randint(seeds[6], (CAP,), 0, 4) < 3).astype(jnp.int32), jax.random.fold_in(seeds[6], 1), 0, 1)
    kept = with_ends((jax.random.randint(seeds[7], (NT, NH, 4), 0, 2) < 1).astype(jnp.int32), jax.random.fold_in(seeds[7], 1), 0, 1)
    return {"queries": queries, "keys": keys, "values": values, "grad_out": grad_out, "caption_keys": caption_keys, "caption_values": caption_values, "caption_mask": caption_mask, "kept": kept}


def split_heads(array):
    return array.reshape(array.shape[:-1] + (HEADS, HD)).astype(jnp.float32)

def round_half(array):
    return lax.optimization_barrier(array.astype(jnp.bfloat16)).astype(jnp.float32)

def padded(array):
    return jnp.pad(array, ((1, 1), (1, 1)) + ((0, 0),) * (array.ndim - 2))

def reference(queries, keys, values, grad_out, caption_keys, caption_values, caption_mask, kept):
    score_scale = 1.0 / math.sqrt(HD)
    time_grid = jnp.arange(NT, dtype=jnp.int32)[:, None] + jnp.zeros((1, NH), jnp.int32)
    band_grid = jnp.arange(NH, dtype=jnp.int32)[None, :] + jnp.zeros((NT, 1), jnp.int32)
    inside = jnp.stack([time_grid > 0, time_grid < NT - 1, band_grid > 0, band_grid < NH - 1], axis=-1)
    linked = (kept > 0) & inside
    padded_keys = padded(keys)
    padded_values = padded(values)
    caption_key_heads = split_heads(caption_keys)
    caption_value_heads = split_heads(caption_values)
    caption_usable = caption_mask > 0
    offsets = ((1, 1), (0, 1), (2, 1), (1, 0), (1, 2))

    def forward_tile(totals, tile_index):
        time_at = tile_index // NH
        band_at = tile_index % NH
        key_rows = jnp.concatenate([padded_keys[time_at + slot_time, band_at + slot_band] for slot_time, slot_band in offsets], axis=0)
        value_rows = jnp.concatenate([padded_values[time_at + slot_time, band_at + slot_band] for slot_time, slot_band in offsets], axis=0)
        key_heads = jnp.concatenate([split_heads(key_rows), caption_key_heads], axis=0)
        value_heads = jnp.concatenate([split_heads(value_rows), caption_value_heads], axis=0)
        usable = jnp.concatenate([jnp.ones((TILE,), jnp.bool_)] + [jnp.full((TILE,), linked[time_at, band_at, direction]) for direction in range(4)] + [caption_usable])
        query_heads = split_heads(queries[time_at, band_at])
        cotangent = split_heads(grad_out[time_at, band_at])
        scores = jnp.einsum('rhd,khd->hrk', query_heads, key_heads) * score_scale
        scores = jnp.where(usable, scores, -jnp.inf)
        row_top = lax.optimization_barrier(jnp.max(scores, axis=-1, keepdims=True))
        log_total = row_top + jnp.log(lax.optimization_barrier(jnp.sum(jnp.exp(scores - row_top), axis=-1, keepdims=True)))
        weights = jnp.exp(scores - log_total)
        weights_half = round_half(weights)
        out_tile = jnp.einsum('hrk,khd->rhd', weights_half, value_heads).reshape(TILE, D).astype(jnp.bfloat16)
        row_delta = lax.optimization_barrier(jnp.sum(split_heads(out_tile) * cotangent, axis=-1)).T[:, :, None]
        dweights = jnp.einsum('rhd,khd->hrk', cotangent, value_heads)
        dscores = round_half(weights * (dweights - row_delta))
        dquery = (jnp.einsum('hrk,khd->rhd', dscores, key_heads) * score_scale).reshape(TILE, D).astype(jnp.bfloat16)
        caption_dk = jnp.einsum('hrk,rhd->khd', dscores[:, :, 5 * TILE:], query_heads) * score_scale
        caption_dv = jnp.einsum('hrk,rhd->khd', weights_half[:, :, 5 * TILE:], cotangent)
        totals = (totals[0] + caption_dk.reshape(CAP, D), totals[1] + caption_dv.reshape(CAP, D))
        return (totals, (out_tile, dquery, log_total[:, :, 0], row_delta[:, :, 0]))
    start_totals = (jnp.zeros((CAP, D), jnp.float32), jnp.zeros((CAP, D), jnp.float32))
    tile_numbers = jnp.arange(NT * NH, dtype=jnp.int32)
    caption_sums, per_tile = lax.scan(forward_tile, start_totals, tile_numbers)
    attended = per_tile[0].reshape(NT, NH, TILE, D)
    query_grad = per_tile[1].reshape(NT, NH, TILE, D)
    log_totals = per_tile[2].reshape(NT, NH, HEADS, TILE)
    row_deltas = per_tile[3].reshape(NT, NH, HEADS, TILE)
    padded_queries = padded(queries)
    padded_grads = padded(grad_out)
    padded_totals = padded(log_totals)
    padded_deltas = padded(row_deltas)
    padded_links = padded(linked)
    sources = ((2, 1, 0), (0, 1, 1), (1, 2, 2), (1, 0, 3))

    def key_tile(tile_index):
        time_at = tile_index // NH
        band_at = tile_index % NH
        key_heads = split_heads(keys[time_at, band_at])
        value_heads = split_heads(values[time_at, band_at])
        query_stack = jnp.stack([queries[time_at, band_at]] + [padded_queries[time_at + slot_time, band_at + slot_band] for slot_time, slot_band, direction in sources])
        grad_stack = jnp.stack([grad_out[time_at, band_at]] + [padded_grads[time_at + slot_time, band_at + slot_band] for slot_time, slot_band, direction in sources])
        total_stack = jnp.stack([log_totals[time_at, band_at]] + [padded_totals[time_at + slot_time, band_at + slot_band] for slot_time, slot_band, direction in sources])
        delta_stack = jnp.stack([row_deltas[time_at, band_at]] + [padded_deltas[time_at + slot_time, band_at + slot_band] for slot_time, slot_band, direction in sources])
        usable = jnp.stack([jnp.array(True)] + [padded_links[time_at + slot_time, band_at + slot_band, direction] for slot_time, slot_band, direction in sources])
        query_heads = split_heads(query_stack)
        cotangent = split_heads(grad_stack)
        scores = jnp.einsum('nrhd,khd->nhrk', query_heads, key_heads) * score_scale
        weights = jnp.where(usable[:, None, None, None], jnp.exp(scores - total_stack[..., None]), 0.0)
        weights_half = round_half(weights)
        dweights = jnp.einsum('nrhd,khd->nhrk', cotangent, value_heads)
        dscores = round_half(weights * (dweights - delta_stack[..., None]))
        dkey = jnp.einsum('nhrk,nrhd->khd', dscores, query_heads) * score_scale
        dvalue = jnp.einsum('nhrk,nrhd->khd', weights_half, cotangent)
        return (dkey.reshape(TILE, D).astype(jnp.bfloat16), dvalue.reshape(TILE, D).astype(jnp.bfloat16))
    key_grad, value_grad = lax.map(key_tile, tile_numbers)
    key_grad = key_grad.reshape(NT, NH, TILE, D)
    value_grad = value_grad.reshape(NT, NH, TILE, D)
    return (attended, query_grad, key_grad, value_grad, caption_sums[0].astype(jnp.bfloat16), caption_sums[1].astype(jnp.bfloat16))
```

```python
import functools
import math

import jax
import jax.numpy as jnp
from jax import lax
from jax.experimental import pallas as pl
from jax.experimental.pallas import tpu as pltpu
from jax.sharding import PartitionSpec as P

HD = 128
NEG = -1e30
F32 = jnp.float32
BF16 = jnp.bfloat16
MESH = pl.DeviceIdType.MESH


class Plan:
    def __init__(self, mesh_shape, tile, cap, heads):
        self.pairs = mesh_shape["tm"] // 2
        self.bands = mesh_shape["height"]
        self.tile, self.cap, self.heads = tile, cap, heads
        self.group = heads // 2
        self.sides = 1 if self.bands == 2 else 2
        self.lo_side = [tile * (1 + j) for j in range(self.sides)]
        self.lo = tile * (1 + self.sides)
        self.hi = self.lo + tile
        self.caps = self.hi + tile
        self.hi_side = [self.caps + cap + tile * j for j in range(self.sides)]
        self.next = self.caps + cap + tile * self.sides
        self.rows = self.next + tile
        self.span = self.caps + cap
        self.inside = self.pairs == 2 and self.bands == 2 and cap % 64 == 0
        self.part = cap // 4
        self.kinds = {}

    def opposite(self, j):
        return 0 if self.sides == 1 else 1 - j

    def number(self, kind, i):
        base = self.kinds.setdefault(kind, len(self.kinds))
        return base * self.group + i


def kernel(plan, scale, q_in, k_in, v_in, g_in, ck_in, cv_in, mask_ref, kept_ref,
           o_att, o_dq, o_dk, o_dv, o_ck, o_cv,
           kb, vb, qb, gb, links, acc, caps, cs, cr, cp, crv, fp, fs, ats,
           local_sem, send_sem, recv_sem):
    T, G, C = plan.tile, plan.group, plan.cap
    tm, band, head = lax.axis_index("tm"), lax.axis_index("height"), lax.axis_index("head")
    s, k = lax.rem(tm, 2), lax.div(tm, 2)
    up_ok, down_ok = k < plan.pairs - 1, k > 0
    partner = (tm + 1 - 2 * s, band, head)
    above, below = (tm + 2, band, head), (tm - 2, band, head)
    if plan.sides == 1:
        side_dev = [(tm, 1 - band, head)]
        side_ok = [None]
    else:
        side_dev = [(tm, band - 1, head), (tm, band + 1, head)]
        side_ok = [band > 0, band < plan.bands - 1]

    def when(ok, fn):
        if ok is None:
            fn()
        else:
            pl.when(ok)(fn)

    def both(a, b):
        return b if a is None else a & b

    def mine(i):
        return pl.ds(pl.multiple_of((s * G + i) * HD, HD), HD)

    def his(i):
        return pl.ds(pl.multiple_of(((1 - s) * G + i) * HD, HD), HD)

    def rows(start, size=T):
        return pl.ds(pl.multiple_of(start, 16), size)

    own_slot, his_slot = rows(plan.lo + s * T), rows(plan.lo + (1 - s) * T)

    def side_slot(j, t):
        return rows(plan.lo_side[j] + t * (plan.hi_side[j] - plan.lo_side[j]))

    def remote(kind, i, src, dst, dev):
        n = plan.number(kind, i)
        return pltpu.make_async_remote_copy(
            src_ref=src, dst_ref=dst, send_sem=send_sem.at[n], recv_sem=recv_sem.at[n],
            device_id=dev, device_id_type=MESH)

    sends = []

    def start(ok, copy):
        when(ok, copy.start)
        sends.append((ok, copy))

    own_kv, own_qg = [], []
    for i in range(G):
        group = [
            (k_in.at[0, 0, :, mine(i)], kb.at[i, own_slot]),
            (v_in.at[0, 0, :, mine(i)], vb.at[i, own_slot]),
            (q_in.at[0, 0, :, mine(i)], qb.at[i, rows(s * T)]),
            (g_in.at[0, 0, :, mine(i)], gb.at[i, rows(s * T)]),
            (ck_in.at[:, mine(i)], kb.at[i, pl.ds(plan.caps, C)]),
            (cv_in.at[:, mine(i)], vb.at[i, pl.ds(plan.caps, C)]),
        ]
        made = [pltpu.make_async_copy(a, b, local_sem.at[6 * i + n]) for n, (a, b) in enumerate(group)]
        for copy in made:
            copy.start()
        own_kv.append(made[:2])
        own_qg.append(made[2:])

    def clear(at, rows_at):
        for i in range(G):
            kb[i, pl.ds(at, T)] = jnp.zeros((T, HD), BF16)
            vb[i, pl.ds(at, T)] = jnp.zeros((T, HD), BF16)
            cr[i, pl.ds(rows_at, T)] = jnp.zeros((T, 2 * HD), BF16)

    pl.when(k == 0)(lambda: clear(0, T))
    pl.when(k == plan.pairs - 1)(lambda: clear(plan.next, 0))
    for j in range(plan.sides):
        if side_ok[j] is not None:
            def clear_side(j=j):
                clear(plan.lo_side[j], 2 * T + 2 * T * j)
                clear(plan.hi_side[j], 3 * T + 2 * T * j)
            pl.when(jnp.logical_not(side_ok[j]))(clear_side)

    time_ok = [tm > 0, tm < 2 * plan.pairs - 1]
    for row in range(2 + plan.sides):
        if row < 2:
            linked = (kept_ref[0, 0, row] > 0) & time_ok[row]
        elif plan.sides == 1:
            linked = kept_ref[0, 0, 3 - band] > 0
        else:
            linked = (kept_ref[0, 0, row] > 0) & side_ok[row - 2]
        links[s, pl.ds(row, 1), :] = jnp.broadcast_to(
            jnp.where(linked, 0.0, NEG).astype(F32), (1, 128))

    barrier = pltpu.get_barrier_semaphore()
    peers = [(None, partner), (up_ok, above), (down_ok, below)]
    peers += [(side_ok[j], side_dev[j]) for j in range(plan.sides)]
    if plan.inside:
        across = lax.rem(tm + 2, 4)
        mates = [(tm, 1 - band, head), (across, band, head), (across, 1 - band, head)]
        peers.append((None, mates[2]))
    for ok, dev in peers:
        when(ok, functools.partial(pl.semaphore_signal, barrier, inc=1, device_id=dev,
                                   device_id_type=MESH))
    pl.semaphore_wait(barrier, sum(1 if ok is None else ok.astype(jnp.int32) for ok, _ in peers))

    link_copy = remote("link", 0, links.at[s], links.at[s], partner)
    start(None, link_copy)
    swap_kv, swap_qg = [], []
    for i in range(G):
        made = [remote("k", i, k_in.at[0, 0, :, his(i)], kb.at[i, own_slot], partner),
                remote("v", i, v_in.at[0, 0, :, his(i)], vb.at[i, own_slot], partner)]
        for copy in made:
            start(None, copy)
        swap_kv.append(made)
    for i in range(G):
        made = [remote("q", i, q_in.at[0, 0, :, his(i)], qb.at[i, rows(s * T)], partner),
                remote("g", i, g_in.at[0, 0, :, his(i)], gb.at[i, rows(s * T)], partner)]
        for copy in made:
            start(None, copy)
        swap_qg.append(made)

    up, down = [], []
    side_first = [[] for _ in range(plan.sides)]
    side_second = [[] for _ in range(plan.sides)]
    for i in range(G):
        up.append([remote("up" + n, i, b.at[i, pl.ds(plan.hi, T)], b.at[i, pl.ds(0, T)], above)
                   for n, b in (("k", kb), ("v", vb))])
        down.append([remote("down" + n, i, b.at[i, pl.ds(plan.lo, T)], b.at[i, pl.ds(plan.next, T)], below)
                     for n, b in (("k", kb), ("v", vb))])
        for j in range(plan.sides):
            o = plan.opposite(j)
            side_first[j].append([
                remote("first%d%s" % (o, n), i, b.at[i, own_slot], b.at[i, side_slot(o, s)], side_dev[j])
                for n, b in (("k", kb), ("v", vb))])
            side_second[j].append([
                remote("second%d%s" % (o, n), i, b.at[i, his_slot], b.at[i, side_slot(o, 1 - s)], side_dev[j])
                for n, b in (("k", kb), ("v", vb))])

    def begin(ok, pair):
        def go():
            for copy in pair:
                copy.start()
        when(ok, go)

    for i in range(G):
        for copy in own_kv[i]:
            copy.wait()
        begin(up_ok & (s == 1), up[i])
        begin(down_ok & (s == 0), down[i])
        for j in range(plan.sides):
            begin(side_ok[j], side_first[j][i])
    for i in range(G):
        for copy in swap_kv[i]:
            copy.wait_recv()
        begin(up_ok & (s == 0), up[i])
        begin(down_ok & (s == 1), down[i])
        for j in range(plan.sides):
            begin(side_ok[j], side_second[j][i])
    for i in range(G):
        sends.extend((up_ok, c) for c in up[i])
        sends.extend((down_ok, c) for c in down[i])
        for j in range(plan.sides):
            sends.extend((side_ok[j], c) for c in side_first[j][i] + side_second[j][i])

    def arrived(ok, pair):
        def go():
            for copy in pair:
                copy.wait_recv()
        when(ok, go)

    link_copy.wait_recv()
    cap_off = jnp.where(mask_ref[...] > 0, 0.0, NEG).astype(F32)
    zero_off = jnp.zeros((1, T), F32)

    def row_of(t, r):
        return links[t, r:r + 1, :]

    side_rows = range(2, 2 + plan.sides)
    offsets = [
        jnp.concatenate([row_of(0, 0)] + [row_of(0, r) for r in side_rows]
                        + [zero_off, row_of(0, 1), cap_off], axis=1),
        jnp.concatenate([row_of(1, 0), zero_off, cap_off]
                        + [row_of(1, r) for r in side_rows] + [row_of(1, 1)], axis=1),
    ]

    def dot(a, b, dims):
        return lax.dot_general(a, b, (dims, ((), ())), preferred_element_type=F32)

    last_recv = []
    returns = {}

    def attend(i):
        for copy in own_qg[i]:
            copy.wait()
        for copy in swap_qg[i]:
            copy.wait_recv()
        arrived(down_ok, up[i])
        arrived(up_ok, down[i])
        for j in range(plan.sides):
            arrived(side_ok[j], side_first[plan.opposite(j)][i] + side_second[plan.opposite(j)][i])
        grads = []
        for t in range(2):
            span = pl.ds(0 if t == 0 else plan.lo, plan.span)
            keys, values = kb[i, span, :], vb[i, span, :]
            query, grad = qb[i, pl.ds(t * T, T), :], gb[i, pl.ds(t * T, T), :]
            scores = dot(query, keys, ((1,), (1,))) * scale + offsets[t]
            top = jnp.max(scores, axis=-1, keepdims=True)
            weights = jnp.exp(scores - top)
            weights = weights * (1.0 / jnp.sum(weights, axis=-1, keepdims=True))
            half = weights.astype(BF16)
            out = dot(half, values, ((1,), (0,))).astype(BF16)
            ats[i, 0, pl.ds(t * T, T), :] = out
            delta = jnp.sum(out.astype(F32) * grad.astype(F32), axis=-1, keepdims=True)
            dweights = dot(grad, values, ((1,), (1,)))
            dscores = (weights * (dweights - delta)).astype(BF16)
            ats[i, 1, pl.ds(t * T, T), :] = (dot(dscores, keys, ((1,), (0,))) * scale).astype(BF16)
            dk = dot(dscores, query, ((0,), (0,))) * scale
            dv = dot(half, grad, ((0,), (0,)))
            grads.append(jnp.concatenate([dk, dv], axis=1))
        made = [remote("att", i, ats.at[i, 0, rows((1 - s) * T)], o_att.at[0, 0, :, mine(i)], partner),
                remote("dq", i, ats.at[i, 1, rows((1 - s) * T)], o_dq.at[0, 0, :, mine(i)], partner)]
        for copy in made:
            start(None, copy)
            last_recv.append(copy)
        low, high = grads
        mid = plan.lo
        cs[i, pl.ds(0, T), :] = low[:T].astype(BF16)
        cs[i, pl.ds(T, T), :] = high[plan.span - T:].astype(BF16)
        for j in range(plan.sides):
            at = 2 * T + 2 * T * j
            cs[i, pl.ds(at, T), :] = low[plan.lo_side[j]:plan.lo_side[j] + T].astype(BF16)
            hs = plan.hi_side[j] - mid
            cs[i, pl.ds(at + T, T), :] = high[hs:hs + T].astype(BF16)
        to_below = remote("rb", i, cs.at[i, pl.ds(0, T)], cr.at[i, pl.ds(0, T)], below)
        to_above = remote("ra", i, cs.at[i, pl.ds(T, T)], cr.at[i, pl.ds(T, T)], above)
        start(down_ok, to_below)
        start(up_ok, to_above)
        to_side = []
        for j in range(plan.sides):
            o = plan.opposite(j)
            copy = remote("rs%d" % o, i, cs.at[i, pl.ds(2 * T + 2 * T * j, 2 * T)],
                          cr.at[i, pl.ds(2 * T + 2 * T * o, 2 * T)], side_dev[j])
            start(side_ok[j], copy)
            to_side.append(copy)
        shared = low[mid:] + high[:plan.span - mid]
        tail = shared[2 * T:]
        if plan.inside:
            caps[i] = tail
            cp[i] = tail.astype(BF16)
            numbers = [2 * k + 1 - band, 2 * (1 - k) + band, 2 * (1 - k) + 1 - band]
            rs = [remote("cr%d" % n, i, cp.at[i, rows(numbers[n] * plan.part, plan.part)],
                         crv.at[i, n], mates[n]) for n in range(3)]
            for copy in rs:
                start(None, copy)
        else:
            rs = []
            o_ck[:, i * HD:(i + 1) * HD] = tail[:, :HD]
            o_cv[:, i * HD:(i + 1) * HD] = tail[:, HD:]
        acc[i] = shared[:2 * T]
        o_att[0, 0, :, mine(i)] = ats[i, 0, rows(s * T), :]
        o_dq[0, 0, :, mine(i)] = ats[i, 1, rows(s * T), :]
        returns[i] = (to_below, to_above, to_side, rs)

    def finish(i):
        to_below, to_above, to_side, rs = returns[i]
        arrived(up_ok, [to_below])
        arrived(down_ok, [to_above])
        for j in range(plan.sides):
            arrived(side_ok[j], [to_side[plan.opposite(j)]])
        for t in range(2):
            total = acc[i, pl.ds(t * T, T), :] + cr[i, pl.ds((1 - t) * T, T), :].astype(F32)
            for j in range(plan.sides):
                total = total + cr[i, pl.ds(2 * T + 2 * T * j + t * T, T), :].astype(F32)
            fs[i, pl.ds(t * T, T), :] = total.astype(BF16)
        made = [remote("dk", i, fs.at[i, rows((1 - s) * T), pl.ds(0, HD)], o_dk.at[0, 0, :, mine(i)], partner),
                remote("dv", i, fs.at[i, rows((1 - s) * T), pl.ds(HD, HD)], o_dv.at[0, 0, :, mine(i)], partner)]
        for copy in made:
            start(None, copy)
            last_recv.append(copy)
        o_dk[0, 0, :, mine(i)] = fs[i, rows(s * T), :HD]
        o_dv[0, 0, :, mine(i)] = fs[i, rows(s * T), HD:]

    cap_parts = {}

    def caption(i):
        if not plan.inside:
            return
        for copy in returns[i][3]:
            copy.wait_recv()
        at = rows((2 * k + band) * plan.part, plan.part)
        total = caps[i, at, :]
        for n in range(3):
            total = total + crv[i, n].astype(F32)
        fp[i] = total.astype(BF16)
        k_src, v_src = fp.at[i, :, pl.ds(0, HD)], fp.at[i, :, pl.ds(HD, HD)]
        ahead = []
        for n, dev in enumerate([partner] + mates):
            pair = [remote("fk%d" % n, i, k_src, o_ck.at[at, mine(i)], dev),
                    remote("fv%d" % n, i, v_src, o_cv.at[at, mine(i)], dev)]
            for copy in pair:
                start(None, copy)
            if n == 0:
                cap_parts[i] = pair
            else:
                last_recv.extend(pair)
        o_ck[at, mine(i)] = fp[i, :, :HD]
        o_cv[at, mine(i)] = fp[i, :, HD:]

    def pass_on(i):
        if not plan.inside:
            return
        for copy in cap_parts[i]:
            copy.wait_recv()
        at = rows((2 * k + band) * plan.part, plan.part)
        for n, dev in enumerate(mates):
            pair = [remote("pk%d" % n, i, o_ck.at[at, his(i)], o_ck.at[at, his(i)], dev),
                    remote("pv%d" % n, i, o_cv.at[at, his(i)], o_cv.at[at, his(i)], dev)]
            for copy in pair:
                start(None, copy)
                last_recv.append(copy)

    for i in range(G):
        attend(i)
        if i >= 1:
            finish(i - 1)
            caption(i - 1)
        if i >= 2:
            pass_on(i - 2)
    finish(G - 1)
    caption(G - 1)
    for i in range(max(G - 2, 0), G):
        pass_on(i)
    for copy in last_recv:
        copy.wait_recv()
    for ok, copy in sends:
        when(ok, copy.wait_send)


def kinds_of(plan):
    names = ["link", "k", "v", "q", "g", "att", "dq", "dk", "dv", "rb", "ra"]
    names += [d + n for d in ("up", "down") for n in "kv"]
    for j in range(plan.sides):
        names += ["%s%d%s" % (d, j, n) for d in ("first", "second") for n in "kv"] + ["rs%d" % j]
    if plan.inside:
        names += ["cr%d" % n for n in range(3)]
        names += ["%s%d" % (d, n) for d in ("fk", "fv") for n in range(4)]
        names += ["%s%d" % (d, n) for d in ("pk", "pv") for n in range(3)]
    return names


def body(mesh_shape, queries, keys, values, grad_out, caption_keys, caption_values, caption_mask, kept):
    T, C = queries.shape[2], caption_keys.shape[0]
    width = queries.shape[3]
    plan = Plan(mesh_shape, T, C, width // HD)
    for name in kinds_of(plan):
        plan.number(name, 0)
    G = plan.group
    count = len(plan.kinds) * G
    tile_out = jax.ShapeDtypeStruct(queries.shape, BF16)
    cap_out = (jax.ShapeDtypeStruct((C, width), BF16) if plan.inside
               else jax.ShapeDtypeStruct((C, G * HD), F32))
    hbm = pl.BlockSpec(memory_space=pltpu.HBM)
    vmem = pl.BlockSpec(memory_space=pltpu.VMEM)
    smem = pl.BlockSpec(memory_space=pltpu.SMEM)
    cap_rows = C if plan.inside else 16
    part = plan.part if plan.inside else 16
    side_rows = 2 * T + 2 * T * plan.sides
    outs = pl.pallas_call(
        functools.partial(kernel, plan, 1.0 / math.sqrt(HD)),
        out_shape=(tile_out,) * 4 + (cap_out,) * 2,
        in_specs=[hbm] * 6 + [vmem, smem],
        out_specs=(vmem,) * 6,
        scratch_shapes=[
            pltpu.VMEM((G, plan.rows, HD), BF16),
            pltpu.VMEM((G, plan.rows, HD), BF16),
            pltpu.VMEM((G, 2 * T, HD), BF16),
            pltpu.VMEM((G, 2 * T, HD), BF16),
            pltpu.VMEM((2, 8, 128), F32),
            pltpu.VMEM((G, 2 * T, 2 * HD), F32),
            pltpu.VMEM((G, cap_rows, 2 * HD), F32),
            pltpu.VMEM((G, side_rows, 2 * HD), BF16),
            pltpu.VMEM((G, side_rows, 2 * HD), BF16),
            pltpu.VMEM((G, cap_rows, 2 * HD), BF16),
            pltpu.VMEM((G, 3, part, 2 * HD), BF16),
            pltpu.VMEM((G, part, 2 * HD), BF16),
            pltpu.VMEM((G, 2 * T, 2 * HD), BF16),
            pltpu.VMEM((G, 2, 2 * T, HD), BF16),
            pltpu.SemaphoreType.DMA((6 * G,)),
            pltpu.SemaphoreType.DMA((count,)),
            pltpu.SemaphoreType.DMA((count,)),
        ],
        compiler_params=pltpu.CompilerParams(
            collective_id=0, has_side_effects=True, vmem_limit_bytes=40 * 1024 * 1024),
    )(queries, keys, values, grad_out, caption_keys, caption_values,
      caption_mask.reshape(1, C), kept)
    if plan.inside:
        return outs
    at = lax.rem(lax.axis_index("tm"), 2) * (G * HD)
    summed = [lax.dynamic_update_slice(jnp.zeros((C, width), F32), part, (0, at)) for part in outs[4:]]
    summed = lax.psum(tuple(summed), ("tm", "height"))
    return outs[:4] + tuple(x.astype(BF16) for x in summed)


def solution(mesh):
    tiles = P("tm", "height", None, "head")
    caption = P(None, "head")
    return jax.shard_map(
        functools.partial(body, dict(mesh.shape)),
        mesh=mesh,
        in_specs=(tiles,) * 4 + (caption,) * 2 + (P(), P("tm", "height", None)),
        out_specs=(tiles,) * 4 + (caption,) * 2,
        check_vma=False,
    )
```

```python
import functools
import math

import jax
import jax.numpy as jnp
from jax import lax
from jax.experimental import pallas as pl
from jax.experimental.pallas import tpu as pltpu
from jax.sharding import PartitionSpec as P

HD = 128
NEG = -1e30
F32 = jnp.float32
BF16 = jnp.bfloat16
ORDER = ["att", "dq", "dk", "dv", "ck", "cv"]
MESH = pl.DeviceIdType.MESH


class Plan:
    def __init__(self, mesh_shape, tile, cap, heads):
        self.pairs = mesh_shape["tm"] // 2
        self.bands = mesh_shape["height"]
        self.tile, self.cap, self.heads = tile, cap, heads
        self.group = heads // 2
        self.sides = 1 if self.bands == 2 else 2
        self.lo_side = [tile * (1 + j) for j in range(self.sides)]
        self.lo = tile * (1 + self.sides)
        self.hi = self.lo + tile
        self.caps = self.hi + tile
        self.hi_side = [self.caps + cap + tile * j for j in range(self.sides)]
        self.next = self.caps + cap + tile * self.sides
        self.rows = self.next + tile
        self.span = self.caps + cap
        self.inside = self.pairs == 2 and self.bands == 2 and cap % 64 == 0
        self.part = cap // 4
        self.kinds = {}

    def opposite(self, j):
        return 0 if self.sides == 1 else 1 - j

    def number(self, kind, i):
        base = self.kinds.setdefault(kind, len(self.kinds))
        return base * self.group + i


def kernel(plan, scale, *refs):
    hbm_in, (mask_ref, kept_ref), hbm_out = refs[:6], refs[6:8], refs[8:14]
    q_in, k_in, v_in, g_in, ck_in, cv_in = here_in = refs[14:20]
    o_att, o_dq, o_dk, o_dv, o_ck, o_cv = here_out = refs[20:26]
    (kb, vb, qb, gb, links, acc, caps, cs, cr, cp, crv, fp, fs, ats,
     stage_sem, local_sem, send_sem, recv_sem) = refs[26:]
    T, G, C = plan.tile, plan.group, plan.cap
    tm, band, head = lax.axis_index("tm"), lax.axis_index("height"), lax.axis_index("head")
    s, k = lax.rem(tm, 2), lax.div(tm, 2)
    up_ok, down_ok = k < plan.pairs - 1, k > 0
    partner = (tm + 1 - 2 * s, band, head)
    above, below = (tm + 2, band, head), (tm - 2, band, head)
    if plan.sides == 1:
        side_dev = [(tm, 1 - band, head)]
        side_ok = [None]
    else:
        side_dev = [(tm, band - 1, head), (tm, band + 1, head)]
        side_ok = [band > 0, band < plan.bands - 1]

    def when(ok, fn):
        if ok is None:
            fn()
        else:
            pl.when(ok)(fn)

    def both(a, b):
        return b if a is None else a & b

    def mine(i):
        return pl.ds(pl.multiple_of((s * G + i) * HD, HD), HD)

    def his(i):
        return pl.ds(pl.multiple_of(((1 - s) * G + i) * HD, HD), HD)

    def rows(start, size=T):
        return pl.ds(pl.multiple_of(start, 16), size)

    own_slot, his_slot = rows(plan.lo + s * T), rows(plan.lo + (1 - s) * T)

    def side_slot(j, t):
        return rows(plan.lo_side[j] + t * (plan.hi_side[j] - plan.lo_side[j]))

    def remote(kind, i, src, dst, dev):
        n = plan.number(kind, i)
        return pltpu.make_async_remote_copy(
            src_ref=src, dst_ref=dst, send_sem=send_sem.at[n], recv_sem=recv_sem.at[n],
            device_id=dev, device_id_type=MESH)

    sends = []

    def start(ok, copy):
        when(ok, copy.start)
        sends.append((ok, copy))

    staged = [pltpu.make_async_copy(hbm_in[n], here_in[n], stage_sem.at[n]) for n in range(6)]
    for n in (1, 2, 0, 3, 4, 5):
        staged[n].start()

    own_kv, own_qg = [], []
    for i in range(G):
        group = [
            (k_in.at[0, 0, :, mine(i)], kb.at[i, own_slot]),
            (v_in.at[0, 0, :, mine(i)], vb.at[i, own_slot]),
            (q_in.at[0, 0, :, mine(i)], qb.at[i, rows(s * T)]),
            (g_in.at[0, 0, :, mine(i)], gb.at[i, rows(s * T)]),
            (ck_in.at[:, mine(i)], kb.at[i, pl.ds(plan.caps, C)]),
            (cv_in.at[:, mine(i)], vb.at[i, pl.ds(plan.caps, C)]),
        ]
        made = [pltpu.make_async_copy(a, b, local_sem.at[6 * i + n]) for n, (a, b) in enumerate(group)]
        own_kv.append(made[:2])
        own_qg.append(made[2:])

    def clear(at, rows_at):
        for i in range(G):
            kb[i, pl.ds(at, T)] = jnp.zeros((T, HD), BF16)
            vb[i, pl.ds(at, T)] = jnp.zeros((T, HD), BF16)
            cr[i, pl.ds(rows_at, T)] = jnp.zeros((T, 2 * HD), BF16)

    pl.when(k == 0)(lambda: clear(0, T))
    pl.when(k == plan.pairs - 1)(lambda: clear(plan.next, 0))
    for j in range(plan.sides):
        if side_ok[j] is not None:
            def clear_side(j=j):
                clear(plan.lo_side[j], 2 * T + 2 * T * j)
                clear(plan.hi_side[j], 3 * T + 2 * T * j)
            pl.when(jnp.logical_not(side_ok[j]))(clear_side)

    time_ok = [tm > 0, tm < 2 * plan.pairs - 1]
    for row in range(2 + plan.sides):
        if row < 2:
            linked = (kept_ref[0, 0, row] > 0) & time_ok[row]
        elif plan.sides == 1:
            linked = kept_ref[0, 0, 3 - band] > 0
        else:
            linked = (kept_ref[0, 0, row] > 0) & side_ok[row - 2]
        links[s, pl.ds(row, 1), :] = jnp.broadcast_to(
            jnp.where(linked, 0.0, NEG).astype(F32), (1, 128))

    barrier = pltpu.get_barrier_semaphore()
    peers = [(None, partner), (up_ok, above), (down_ok, below)]
    peers += [(side_ok[j], side_dev[j]) for j in range(plan.sides)]
    if plan.inside:
        across = lax.rem(tm + 2, 4)
        mates = [(tm, 1 - band, head), (across, band, head), (across, 1 - band, head)]
        peers.append((None, mates[2]))
    for ok, dev in peers:
        when(ok, functools.partial(pl.semaphore_signal, barrier, inc=1, device_id=dev,
                                   device_id_type=MESH))
    pl.semaphore_wait(barrier, sum(1 if ok is None else ok.astype(jnp.int32) for ok, _ in peers))

    link_copy = remote("link", 0, links.at[s], links.at[s], partner)
    start(None, link_copy)
    swap_kv, swap_qg = [], []
    staged[1].wait()
    staged[2].wait()
    for i in range(G):
        made = [remote("k", i, k_in.at[0, 0, :, his(i)], kb.at[i, own_slot], partner),
                remote("v", i, v_in.at[0, 0, :, his(i)], vb.at[i, own_slot], partner)]
        for copy in made:
            start(None, copy)
        swap_kv.append(made)
    for i in range(G):
        for copy in own_kv[i]:
            copy.start()
    staged[0].wait()
    staged[3].wait()
    for i in range(G):
        made = [remote("q", i, q_in.at[0, 0, :, his(i)], qb.at[i, rows(s * T)], partner),
                remote("g", i, g_in.at[0, 0, :, his(i)], gb.at[i, rows(s * T)], partner)]
        for copy in made:
            start(None, copy)
        swap_qg.append(made)
    staged[4].wait()
    staged[5].wait()
    for i in range(G):
        for copy in own_qg[i]:
            copy.start()

    up, down = [], []
    side_first = [[] for _ in range(plan.sides)]
    side_second = [[] for _ in range(plan.sides)]
    for i in range(G):
        up.append([remote("up" + n, i, b.at[i, pl.ds(plan.hi, T)], b.at[i, pl.ds(0, T)], above)
                   for n, b in (("k", kb), ("v", vb))])
        down.append([remote("down" + n, i, b.at[i, pl.ds(plan.lo, T)], b.at[i, pl.ds(plan.next, T)], below)
                     for n, b in (("k", kb), ("v", vb))])
        for j in range(plan.sides):
            o = plan.opposite(j)
            side_first[j].append([
                remote("first%d%s" % (o, n), i, b.at[i, own_slot], b.at[i, side_slot(o, s)], side_dev[j])
                for n, b in (("k", kb), ("v", vb))])
            side_second[j].append([
                remote("second%d%s" % (o, n), i, b.at[i, his_slot], b.at[i, side_slot(o, 1 - s)], side_dev[j])
                for n, b in (("k", kb), ("v", vb))])

    def begin(ok, pair):
        def go():
            for copy in pair:
                copy.start()
        when(ok, go)

    for i in range(G):
        for copy in own_kv[i]:
            copy.wait()
        begin(up_ok & (s == 1), up[i])
        begin(down_ok & (s == 0), down[i])
        for j in range(plan.sides):
            begin(side_ok[j], side_first[j][i])
    for i in range(G):
        for copy in swap_kv[i]:
            copy.wait_recv()
        begin(up_ok & (s == 0), up[i])
        begin(down_ok & (s == 1), down[i])
        for j in range(plan.sides):
            begin(side_ok[j], side_second[j][i])
    for i in range(G):
        sends.extend((up_ok, c) for c in up[i])
        sends.extend((down_ok, c) for c in down[i])
        for j in range(plan.sides):
            sends.extend((side_ok[j], c) for c in side_first[j][i] + side_second[j][i])

    def arrived(ok, pair):
        def go():
            for copy in pair:
                copy.wait_recv()
        when(ok, go)

    link_copy.wait_recv()
    cap_off = jnp.where(mask_ref[...] > 0, 0.0, NEG).astype(F32)
    zero_off = jnp.zeros((1, T), F32)

    def row_of(t, r):
        return links[t, r:r + 1, :]

    side_rows = range(2, 2 + plan.sides)
    offsets = [
        jnp.concatenate([row_of(0, 0)] + [row_of(0, r) for r in side_rows]
                        + [zero_off, row_of(0, 1), cap_off], axis=1),
        jnp.concatenate([row_of(1, 0), zero_off, cap_off]
                        + [row_of(1, r) for r in side_rows] + [row_of(1, 1)], axis=1),
    ]

    def dot(a, b, dims):
        return lax.dot_general(a, b, (dims, ((), ())), preferred_element_type=F32)

    last_recv = {name: [] for name in ORDER}
    returns = {}
    kept_here = {name: [] for name in ORDER}

    def keep(n, i, src, dst):
        copy = pltpu.make_async_copy(src, dst, local_sem.at[6 * i + n])
        copy.start()
        kept_here[ORDER[n]].append(copy.wait)

    def attend(i):
        for copy in own_qg[i]:
            copy.wait()
        for copy in swap_qg[i]:
            copy.wait_recv()
        arrived(down_ok, up[i])
        arrived(up_ok, down[i])
        for j in range(plan.sides):
            arrived(side_ok[j], side_first[plan.opposite(j)][i] + side_second[plan.opposite(j)][i])
        grads = []
        for t in range(2):
            span = pl.ds(0 if t == 0 else plan.lo, plan.span)
            keys, values = kb[i, span, :], vb[i, span, :]
            query, grad = qb[i, pl.ds(t * T, T), :], gb[i, pl.ds(t * T, T), :]
            scores = dot(query, keys, ((1,), (1,))) * scale + offsets[t]
            top = jnp.max(scores, axis=-1, keepdims=True)
            weights = jnp.exp(scores - top)
            weights = weights * (1.0 / jnp.sum(weights, axis=-1, keepdims=True))
            half = weights.astype(BF16)
            out = dot(half, values, ((1,), (0,))).astype(BF16)
            ats[i, 0, pl.ds(t * T, T), :] = out
            delta = jnp.sum(out.astype(F32) * grad.astype(F32), axis=-1, keepdims=True)
            dweights = dot(grad, values, ((1,), (1,)))
            dscores = (weights * (dweights - delta)).astype(BF16)
            ats[i, 1, pl.ds(t * T, T), :] = (dot(dscores, keys, ((1,), (0,))) * scale).astype(BF16)
            dk = dot(dscores, query, ((0,), (0,))) * scale
            dv = dot(half, grad, ((0,), (0,)))
            grads.append(jnp.concatenate([dk, dv], axis=1))
        made = [remote("att", i, ats.at[i, 0, rows((1 - s) * T)], o_att.at[0, 0, :, mine(i)], partner),
                remote("dq", i, ats.at[i, 1, rows((1 - s) * T)], o_dq.at[0, 0, :, mine(i)], partner)]
        for name, copy in zip(("att", "dq"), made):
            start(None, copy)
            last_recv[name].append(copy.wait_recv)
        low, high = grads
        mid = plan.lo
        cs[i, pl.ds(0, T), :] = low[:T].astype(BF16)
        cs[i, pl.ds(T, T), :] = high[plan.span - T:].astype(BF16)
        for j in range(plan.sides):
            at = 2 * T + 2 * T * j
            cs[i, pl.ds(at, T), :] = low[plan.lo_side[j]:plan.lo_side[j] + T].astype(BF16)
            hs = plan.hi_side[j] - mid
            cs[i, pl.ds(at + T, T), :] = high[hs:hs + T].astype(BF16)
        to_below = remote("rb", i, cs.at[i, pl.ds(0, T)], cr.at[i, pl.ds(0, T)], below)
        to_above = remote("ra", i, cs.at[i, pl.ds(T, T)], cr.at[i, pl.ds(T, T)], above)
        start(down_ok, to_below)
        start(up_ok, to_above)
        to_side = []
        for j in range(plan.sides):
            o = plan.opposite(j)
            copy = remote("rs%d" % o, i, cs.at[i, pl.ds(2 * T + 2 * T * j, 2 * T)],
                          cr.at[i, pl.ds(2 * T + 2 * T * o, 2 * T)], side_dev[j])
            start(side_ok[j], copy)
            to_side.append(copy)
        shared = low[mid:] + high[:plan.span - mid]
        tail = shared[2 * T:]
        if plan.inside:
            caps[i] = tail
            cp[i] = tail.astype(BF16)
            numbers = [2 * k + 1 - band, 2 * (1 - k) + band, 2 * (1 - k) + 1 - band]
            rs = [remote("cr%d" % n, i, cp.at[i, rows(numbers[n] * plan.part, plan.part)],
                         crv.at[i, n], mates[n]) for n in range(3)]
            for copy in rs:
                start(None, copy)
        else:
            rs = []
            o_ck[:, i * HD:(i + 1) * HD] = tail[:, :HD]
            o_cv[:, i * HD:(i + 1) * HD] = tail[:, HD:]
        acc[i] = shared[:2 * T]
        keep(0, i, ats.at[i, 0, rows(s * T)], o_att.at[0, 0, :, mine(i)])
        keep(1, i, ats.at[i, 1, rows(s * T)], o_dq.at[0, 0, :, mine(i)])
        returns[i] = (to_below, to_above, to_side, rs)

    def finish(i):
        to_below, to_above, to_side, rs = returns[i]
        arrived(up_ok, [to_below])
        arrived(down_ok, [to_above])
        for j in range(plan.sides):
            arrived(side_ok[j], [to_side[plan.opposite(j)]])
        for t in range(2):
            total = acc[i, pl.ds(t * T, T), :] + cr[i, pl.ds((1 - t) * T, T), :].astype(F32)
            for j in range(plan.sides):
                total = total + cr[i, pl.ds(2 * T + 2 * T * j + t * T, T), :].astype(F32)
            fs[i, pl.ds(t * T, T), :] = total.astype(BF16)
        made = [remote("dk", i, fs.at[i, rows((1 - s) * T), pl.ds(0, HD)], o_dk.at[0, 0, :, mine(i)], partner),
                remote("dv", i, fs.at[i, rows((1 - s) * T), pl.ds(HD, HD)], o_dv.at[0, 0, :, mine(i)], partner)]
        for name, copy in zip(("dk", "dv"), made):
            start(None, copy)
            last_recv[name].append(copy.wait_recv)
        keep(2, i, fs.at[i, rows(s * T), pl.ds(0, HD)], o_dk.at[0, 0, :, mine(i)])
        keep(3, i, fs.at[i, rows(s * T), pl.ds(HD, HD)], o_dv.at[0, 0, :, mine(i)])

    cap_parts = {}

    def caption(i):
        if not plan.inside:
            return
        for copy in returns[i][3]:
            copy.wait_recv()
        at = rows((2 * k + band) * plan.part, plan.part)
        total = caps[i, at, :]
        for n in range(3):
            total = total + crv[i, n].astype(F32)
        fp[i] = total.astype(BF16)
        k_src, v_src = fp.at[i, :, pl.ds(0, HD)], fp.at[i, :, pl.ds(HD, HD)]
        ahead = []
        for n, dev in enumerate([partner] + mates):
            pair = [remote("fk%d" % n, i, k_src, o_ck.at[at, mine(i)], dev),
                    remote("fv%d" % n, i, v_src, o_cv.at[at, mine(i)], dev)]
            for copy in pair:
                start(None, copy)
            if n == 0:
                cap_parts[i] = pair
            else:
                for name, copy in zip(("ck", "cv"), pair):
                    last_recv[name].append(copy.wait_recv)
        keep(4, i, k_src, o_ck.at[at, mine(i)])
        keep(5, i, v_src, o_cv.at[at, mine(i)])

    def pass_on(i):
        if not plan.inside:
            return
        for copy in cap_parts[i]:
            copy.wait_recv()
        at = rows((2 * k + band) * plan.part, plan.part)
        for n, dev in enumerate(mates):
            pair = [remote("pk%d" % n, i, o_ck.at[at, his(i)], o_ck.at[at, his(i)], dev),
                    remote("pv%d" % n, i, o_cv.at[at, his(i)], o_cv.at[at, his(i)], dev)]
            for name, copy in zip(("ck", "cv"), pair):
                start(None, copy)
                last_recv[name].append(copy.wait_recv)

    for i in range(G):
        attend(i)
        if i >= 1:
            finish(i - 1)
            caption(i - 1)
        if i >= 2:
            pass_on(i - 2)
    finish(G - 1)
    caption(G - 1)
    for i in range(max(G - 2, 0), G):
        pass_on(i)
    written = []
    for names in (("att", "dq"), ("dk", "dv"), ("ck", "cv")):
        for name in names:
            for copy in last_recv[name] + kept_here[name]:
                copy()
            n = ORDER.index(name)
            made = pltpu.make_async_copy(here_out[n], hbm_out[n], stage_sem.at[n])
            made.start()
            written.append(made)
    for copy in written:
        copy.wait()
    for ok, copy in sends:
        when(ok, copy.wait_send)


def kinds_of(plan):
    names = ["link", "k", "v", "q", "g", "att", "dq", "dk", "dv", "rb", "ra"]
    names += [d + n for d in ("up", "down") for n in "kv"]
    for j in range(plan.sides):
        names += ["%s%d%s" % (d, j, n) for d in ("first", "second") for n in "kv"] + ["rs%d" % j]
    if plan.inside:
        names += ["cr%d" % n for n in range(3)]
        names += ["%s%d" % (d, n) for d in ("fk", "fv") for n in range(4)]
        names += ["%s%d" % (d, n) for d in ("pk", "pv") for n in range(3)]
    return names


def body(mesh_shape, queries, keys, values, grad_out, caption_keys, caption_values, caption_mask, kept):
    T, C = queries.shape[2], caption_keys.shape[0]
    width = queries.shape[3]
    plan = Plan(mesh_shape, T, C, width // HD)
    for name in kinds_of(plan):
        plan.number(name, 0)
    G = plan.group
    count = len(plan.kinds) * G
    tile_out = jax.ShapeDtypeStruct(queries.shape, BF16)
    cap_out = (jax.ShapeDtypeStruct((C, width), BF16) if plan.inside
               else jax.ShapeDtypeStruct((C, G * HD), F32))
    hbm = pl.BlockSpec(memory_space=pltpu.HBM)
    vmem = pl.BlockSpec(memory_space=pltpu.VMEM)
    smem = pl.BlockSpec(memory_space=pltpu.SMEM)
    cap_rows = C if plan.inside else 16
    part = plan.part if plan.inside else 16
    side_rows = 2 * T + 2 * T * plan.sides
    outs = pl.pallas_call(
        functools.partial(kernel, plan, 1.0 / math.sqrt(HD)),
        out_shape=(tile_out,) * 4 + (cap_out,) * 2,
        in_specs=[hbm] * 6 + [vmem, smem],
        out_specs=(hbm,) * 6,
        scratch_shapes=[pltpu.VMEM(a.shape, BF16) for a in (
            queries, keys, values, grad_out, caption_keys, caption_values)] + [
            pltpu.VMEM(a.shape, a.dtype) for a in (tile_out,) * 4 + (cap_out,) * 2] + [
            pltpu.VMEM((G, plan.rows, HD), BF16),
            pltpu.VMEM((G, plan.rows, HD), BF16),
            pltpu.VMEM((G, 2 * T, HD), BF16),
            pltpu.VMEM((G, 2 * T, HD), BF16),
            pltpu.VMEM((2, 8, 128), F32),
            pltpu.VMEM((G, 2 * T, 2 * HD), F32),
            pltpu.VMEM((G, cap_rows, 2 * HD), F32),
            pltpu.VMEM((G, side_rows, 2 * HD), BF16),
            pltpu.VMEM((G, side_rows, 2 * HD), BF16),
            pltpu.VMEM((G, cap_rows, 2 * HD), BF16),
            pltpu.VMEM((G, 3, part, 2 * HD), BF16),
            pltpu.VMEM((G, part, 2 * HD), BF16),
            pltpu.VMEM((G, 2 * T, 2 * HD), BF16),
            pltpu.VMEM((G, 2, 2 * T, HD), BF16),
            pltpu.SemaphoreType.DMA((6,)),
            pltpu.SemaphoreType.DMA((6 * G,)),
            pltpu.SemaphoreType.DMA((count,)),
            pltpu.SemaphoreType.DMA((count,)),
        ],
        compiler_params=pltpu.CompilerParams(
            collective_id=0, has_side_effects=True, vmem_limit_bytes=58 * 1024 * 1024),
    )(queries, keys, values, grad_out, caption_keys, caption_values,
      caption_mask.reshape(1, C), kept)
    if plan.inside:
        return place(outs)
    at = lax.rem(lax.axis_index("tm"), 2) * (G * HD)
    summed = [lax.dynamic_update_slice(jnp.zeros((C, width), F32), part, (0, at)) for part in outs[4:]]
    summed = lax.psum(tuple(summed), ("tm", "height"))
    return place(outs[:4]) + tuple(x.astype(BF16) for x in summed)


def place_kernel(*refs):
    count = (len(refs) - 1) // 3
    sources, targets, between, sem = refs[:count], refs[count:2 * count], refs[2 * count:3 * count], refs[-1]
    first = [pltpu.make_async_copy(sources[n], between[n], sem.at[0, n]) for n in range(count)]
    second = [pltpu.make_async_copy(between[n], targets[n], sem.at[1, n]) for n in range(count)]
    for copy in first:
        copy.start()
    for n in range(count):
        first[n].wait()
        second[n].start()
    for copy in second:
        copy.wait()


def place(arrays):
    return tuple(pl.pallas_call(
        place_kernel,
        out_shape=tuple(jax.ShapeDtypeStruct(a.shape, a.dtype) for a in arrays),
        in_specs=[pl.BlockSpec(memory_space=pltpu.HBM)] * len(arrays),
        out_specs=(pl.BlockSpec(memory_space=pltpu.HBM),) * len(arrays),
        scratch_shapes=[pltpu.VMEM(a.shape, a.dtype) for a in arrays]
        + [pltpu.SemaphoreType.DMA((2, len(arrays)))],
        compiler_params=pltpu.CompilerParams(vmem_limit_bytes=58 * 1024 * 1024),
    )(*arrays))


def solution(mesh):
    tiles = P("tm", "height", None, "head")
    caption = P(None, "head")
    return jax.shard_map(
        functools.partial(body, dict(mesh.shape)),
        mesh=mesh,
        in_specs=(tiles,) * 4 + (caption,) * 2 + (P(), P("tm", "height", None)),
        out_specs=(tiles,) * 4 + (caption,) * 2,
        check_vma=False,
    )
```
